32 devices in a mesh: row: 2 (over y), col: 16 (over z, x, core).
Axes of the slice: x: 2, y: 2, z: 4, core: 2. Of those that a mesh axis runs over, the one named last changes fastest.
Arguments:
- coefficients: float32 [2, 2, 8, 2048, 512], P(None, None, None, ('row', 'col')), may hold values from -6 to 6
- vertical_modes: float32 [512, 512], replicated, may hold values from -0.25 to 0.25
- mode_slopes: float32 [512, 512], replicated, may hold values from -0.25 to 0.25
- dual_modes: float32 [512, 512], replicated, may hold values from -0.25 to 0.25
- eigenvalues: float32 [512], replicated, may hold values from 0.01 to 10
- velocity: float32 [3, 512, 2048], P(None, 'col'), may hold values from -5 to 5
- gradient: float32 [2, 512], P(None, 'col'), may hold values from 0.2 to 2
- span_wavenumbers: float32 [8], replicated, may hold values from 0 to 2
- implicit_rates: float32 [2], replicated, may hold values from 0.02 to 0.2
- time_step: float32 [], replicated, may hold values from 0.2 to 0.5
Outputs:
- new_coefficients: float32 [2, 2, 8, 2048, 512], P(None, None, None, ('row', 'col'))
The draws below stay inside these ranges and needn't reach their ends.
All inputs are finite; a program needn't handle non-finite values.
Results may differ from the reference program's by a relative error of at most 0.00005.
Values sent between devices are 32-bit elements; how exact they have to be, the bound alone decides.
A program may use at most 128 MiB of HBM per device.

```python
import math
import jax
import jax.numpy as jnp
from jax import lax

NX = 2048
NZ = 512
KY = 8


def shard_levels(stream_key, extent, shards, smallest, largest):
    gain, own = 1.0, jax.random.fold_in(stream_key, 6)
    for axis_at, shards_of in shards:
        steps = jnp.exp(jax.random.uniform(jax.random.fold_in(own, axis_at), (shards_of,), jnp.float32, smallest / len(shards), largest / len(shards)))
        gain = gain * jnp.repeat(steps, extent[axis_at] // shards_of).reshape([-1 if axis == axis_at else 1 for axis in range(len(extent))])
    return gain


def gaussian(rng, extent, deviation, limit, split=(), kind=jnp.bfloat16):
    result = jax.random.normal(rng, extent, jnp.float32) * deviation
    if len(split) > 0:
        result = shard_levels(rng, extent, split, -0.22, 0.18) * result
    return jnp.clip(result, min=-limit, max=limit).astype(kind)


def setup_inputs(seed: int = 0) -> dict:
    streams_of = jax.random.split(jax.random.key(seed), 11)
    coefficients = gaussian(streams_of[0], (2, 2, KY, NX, NZ), 1.0, 6.0, ((3, 32),), jnp.float32)
    vertical_modes = gaussian(streams_of[1], (NZ, NZ), NZ ** -0.5, 0.25, (), jnp.float32)
    mode_slopes = gaussian(streams_of[2], (NZ, NZ), NZ ** -0.5, 0.25, (), jnp.float32)
    dual_modes = gaussian(streams_of[3], (NZ, NZ), NZ ** -0.5, 0.25, (), jnp.float32)
    eigenvalues = jnp.clip(jnp.exp(jax.random.uniform(streams_of[4], (NZ,), jnp.float32, math.log(0.01), math.log(10.0))), 0.01, 10.0)
    velocity = gaussian(streams_of[5], (3, NZ, NX), 1.0, 5.0, ((1, 16),), jnp.float32)
    gradient = jnp.clip(0.2 + 1.8 * jax.random.uniform(streams_of[6], (2, NZ), jnp.float32) ** shard_levels(streams_of[6], (2, NZ), ((1, 16),), -0.2, 0.2), 0.2, 2.0)
    span_wavenumbers = jnp.clip(jax.random.uniform(streams_of[7], (KY,), jnp.float32, 0.0, 2.0), 0.0, 2.0)
    implicit_rates = jnp.clip(jnp.exp(jax.random.uniform(streams_of[8], (2,), jnp.float32, math.log(0.02), math.log(0.2))), 0.02, 0.2)
    time_step = jnp.clip(jax.random.uniform(streams_of[9], (), jnp.float32, 0.2, 0.5), 0.2, 0.5)
    return {"coefficients": coefficients, "vertical_modes": vertical_modes, "mode_slopes": mode_slopes, "dual_modes": dual_modes, "eigenvalues": eigenvalues, "velocity": velocity, "gradient": gradient, "span_wavenumbers": span_wavenumbers, "implicit_rates": implicit_rates, "time_step": time_step}


def reference(coefficients, vertical_modes, mode_slopes, dual_modes, eigenvalues, velocity, gradient, span_wavenumbers, implicit_rates, time_step):
    highest = lax.Precision.HIGHEST
    indices = jnp.arange(NX, dtype=jnp.int32)
    signed = jnp.where(indices < NX // 2, indices, indices - NX)
    zonal_waves = signed.astype(jnp.float32) * (2.0 * math.pi / NX)
    retained = (jnp.abs(signed) <= NX // 3).astype(jnp.float32)
    grid_values = jnp.einsum('scqpj,zj->scqzp', coefficients, vertical_modes, precision=highest)
    grid_slopes = jnp.einsum('scqpj,zj->scqzp', coefficients, mode_slopes, precision=highest)
    values = grid_values[:, 0] + 1j * grid_values[:, 1]
    scalar_grid = jnp.fft.ifft(values, axis=-1, norm="ortho")
    zonal_grad = jnp.fft.ifft(1j * zonal_waves * values, axis=-1, norm="ortho")
    vertical_grad = jnp.fft.ifft(grid_slopes[:, 0] + 1j * grid_slopes[:, 1], axis=-1, norm="ortho")
    zonal_flow = velocity[0]
    span_flow = velocity[1]
    rise_flow = velocity[2]
    span_waves = span_wavenumbers[None, :, None, None]
    advect = zonal_flow * zonal_grad + 1j * span_waves * span_flow * scalar_grid + rise_flow * vertical_grad + rise_flow * gradient[:, None, :, None]
    spectral = jnp.fft.fft(advect, axis=-1, norm="ortho") * retained
    stacked = jnp.stack([jnp.real(spectral), jnp.imag(spectral)], axis=1)
    forcing = jnp.einsum('scqzp,jz->scqpj', stacked, dual_modes, precision=highest)
    denominator = 1.0 + implicit_rates[:, None, None, None, None] * (eigenvalues[None, None, None, None, :] + zonal_waves[None, None, None, :, None] ** 2 + span_wavenumbers[None, None, :, None, None] ** 2)
    return (coefficients - time_step * forcing) / denominator
```

```python
import functools
import math

import jax
import jax.numpy as jnp
import ml_dtypes
import numpy as np
from jax import lax
from jax.experimental import pallas as pl
from jax.experimental.pallas import tpu as pltpu
from jax.sharding import PartitionSpec as P

highest = lax.Precision.HIGHEST
lane_width = 128


def signed_waves(length):
    indices = jnp.arange(length, dtype=jnp.int32)
    return jnp.where(indices < length // 2, indices, indices - length)


def phase_table(row_total, col_total, period, direction):
    left_index = jnp.arange(row_total, dtype=jnp.int32)[:, None]
    right_index = jnp.arange(col_total, dtype=jnp.int32)[None, :]
    angles = (left_index * right_index % period).astype(jnp.float32) * (2.0 * math.pi / period)
    return (jnp.cos(angles), direction * jnp.sin(angles))


def contract(form, left_real, left_imag, right_real, right_imag):
    product_real = jnp.einsum(form, left_real, right_real, precision=highest) - jnp.einsum(
        form, left_imag, right_imag, precision=highest
    )
    product_imag = jnp.einsum(form, left_real, right_imag, precision=highest) + jnp.einsum(
        form, left_imag, right_real, precision=highest
    )
    return (product_real, product_imag)


def twisted(real_in, imag_in, twist_real, twist_imag):
    return (
        real_in * twist_real - imag_in * twist_imag,
        real_in * twist_imag + imag_in * twist_real,
    )


def inverse_transform(real_in, imag_in, length):
    short_size = length // lane_width
    scale = 1.0 / math.sqrt(length)
    short_real, short_imag = phase_table(short_size, short_size, short_size, 1.0)
    twist_real, twist_imag = phase_table(short_size, lane_width, length, 1.0)
    wide_real, wide_imag = phase_table(lane_width, lane_width, lane_width, 1.0)
    middle_real, middle_imag = contract("...ef,ed->...df", real_in, imag_in, short_real, short_imag)
    middle_real, middle_imag = twisted(middle_real, middle_imag, twist_real, twist_imag)
    return contract(
        "...df,fc->...dc", middle_real, middle_imag, wide_real * scale, wide_imag * scale
    )


def forward_transform(real_in, imag_in, length):
    short_size = length // lane_width
    scale = 1.0 / math.sqrt(length)
    short_real, short_imag = phase_table(short_size, short_size, short_size, -1.0)
    twist_real, twist_imag = phase_table(short_size, lane_width, length, -1.0)
    wide_real, wide_imag = phase_table(lane_width, lane_width, lane_width, -1.0)
    middle_real, middle_imag = contract("...dc,cf->...df", real_in, imag_in, wide_real, wide_imag)
    middle_real, middle_imag = twisted(middle_real, middle_imag, twist_real, twist_imag)
    return contract(
        "...df,de->...ef", middle_real, middle_imag, short_real * scale, short_imag * scale
    )


def on_device(
    coefficients,
    vertical_modes,
    mode_slopes,
    dual_modes,
    eigenvalues,
    velocity,
    gradient,
    span_wavenumbers,
    implicit_rates,
    time_step,
):
    row_count = lax.axis_size("row")
    col_count = lax.axis_size("col")
    local_waves = coefficients.shape[3]
    total_points = local_waves * row_count * col_count
    short_size = total_points // lane_width
    first_wave = (lax.axis_index("row") * col_count + lax.axis_index("col")) * local_waves
    signed = signed_waves(total_points)
    zonal_waves = signed.astype(jnp.float32) * (2.0 * math.pi / total_points)
    own_waves = lax.dynamic_slice_in_dim(zonal_waves, first_wave, local_waves)
    value_real = jnp.einsum("sqpj,zj->zsqp", coefficients[:, 0], vertical_modes, precision=highest)
    value_imag = jnp.einsum("sqpj,zj->zsqp", coefficients[:, 1], vertical_modes, precision=highest)
    slope_real = jnp.einsum("sqpj,zj->zsqp", coefficients[:, 0], mode_slopes, precision=highest)
    slope_imag = jnp.einsum("sqpj,zj->zsqp", coefficients[:, 1], mode_slopes, precision=highest)
    fields = (
        lax.all_to_all(value_real, "col", split_axis=0, concat_axis=3, tiled=True),
        lax.all_to_all(value_imag, "col", split_axis=0, concat_axis=3, tiled=True),
        lax.all_to_all(slope_real, "col", split_axis=0, concat_axis=3, tiled=True),
        lax.all_to_all(slope_imag, "col", split_axis=0, concat_axis=3, tiled=True),
    )
    fields = (
        lax.all_to_all(fields[0], "row", split_axis=2, concat_axis=3, tiled=True),
        lax.all_to_all(fields[1], "row", split_axis=2, concat_axis=3, tiled=True),
        lax.all_to_all(fields[2], "row", split_axis=2, concat_axis=3, tiled=True),
        lax.all_to_all(fields[3], "row", split_axis=2, concat_axis=3, tiled=True),
    )
    level_rows = fields[0].shape[0]
    span_rows = fields[0].shape[2]
    grid_shape = (level_rows, 2, span_rows, short_size, lane_width)
    value_real = fields[0].reshape(grid_shape)
    value_imag = fields[1].reshape(grid_shape)
    slope_real = fields[2].reshape(grid_shape)
    slope_imag = fields[3].reshape(grid_shape)
    wave_grid = zonal_waves.reshape(short_size, lane_width)
    scalar_real, scalar_imag = inverse_transform(value_real, value_imag, total_points)
    zonal_real, zonal_imag = inverse_transform(
        -wave_grid * value_imag, wave_grid * value_real, total_points
    )
    rise_real, rise_imag = inverse_transform(slope_real, slope_imag, total_points)
    flow = jnp.swapaxes(velocity.reshape(3, level_rows, lane_width, short_size), -1, -2)
    zonal_flow = flow[0][:, None, None]
    span_flow = flow[1][:, None, None]
    rise_flow = flow[2][:, None, None]
    span_waves = lax.dynamic_slice_in_dim(
        span_wavenumbers, lax.axis_index("row") * span_rows, span_rows
    )[None, None, :, None, None]
    background = jnp.transpose(gradient)[:, :, None, None, None]
    advect_real = (
        zonal_flow * zonal_real
        - span_waves * span_flow * scalar_imag
        + rise_flow * rise_real
        + rise_flow * background
    )
    advect_imag = (
        zonal_flow * zonal_imag + span_waves * span_flow * scalar_real + rise_flow * rise_imag
    )
    spectra_real, spectra_imag = forward_transform(advect_real, advect_imag, total_points)
    retained = (
        (jnp.abs(signed) <= total_points // 3).astype(jnp.float32).reshape(short_size, lane_width)
    )
    flat_shape = (level_rows, 2, span_rows, total_points)
    spectra_real = (spectra_real * retained).reshape(flat_shape)
    spectra_imag = (spectra_imag * retained).reshape(flat_shape)
    returned_real, returned_imag = (
        lax.all_to_all(
            lax.all_to_all(spectra_real, "row", split_axis=3, concat_axis=2, tiled=True),
            "col",
            split_axis=3,
            concat_axis=0,
            tiled=True,
        ),
        lax.all_to_all(
            lax.all_to_all(spectra_imag, "row", split_axis=3, concat_axis=2, tiled=True),
            "col",
            split_axis=3,
            concat_axis=0,
            tiled=True,
        ),
    )
    forcing_real = jnp.einsum("zsqp,jz->sqpj", returned_real, dual_modes, precision=highest)
    forcing_imag = jnp.einsum("zsqp,jz->sqpj", returned_imag, dual_modes, precision=highest)
    forcing = jnp.stack([forcing_real, forcing_imag], 1)
    denominator = 1.0 + implicit_rates[:, None, None, None, None] * (
        eigenvalues[None, None, None, None, :]
        + own_waves[None, None, None, :, None] ** 2
        + span_wavenumbers[None, None, :, None, None] ** 2
    )
    return (coefficients - time_step * forcing) / denominator


def wide_tables(total):
    short = total // lane_width
    points = np.arange(lane_width)[None, :, None]
    waves = np.arange(lane_width)[None, None, :] * short + np.arange(short)[:, None, None]
    angles = (points * waves % total) * (2.0 * math.pi / total)
    scale = 1.0 / math.sqrt(total)
    cosines, sines = np.cos(angles) * scale, np.sin(angles) * scale
    inverse = np.concatenate(
        [
            np.concatenate([cosines, -sines], 2),
            np.concatenate([sines, cosines], 2),
        ],
        1,
    )
    tables = []
    for table in (inverse, np.swapaxes(inverse, 1, 2)):
        high = table.astype(ml_dtypes.bfloat16)
        low = (table - high.astype(np.float64)).astype(ml_dtypes.bfloat16)
        tables += [high, low]
    return tables


def short_transform(values, direction):
    count = len(values)
    if count == 1:
        return values
    even = short_transform(values[0::2], direction)
    odd = short_transform(values[1::2], direction)
    first, second = [], []
    for index in range(count // 2):
        real, imag = odd[index]
        if index == 0:
            pass
        elif 4 * index == count:
            real, imag = (-imag, real) if direction > 0 else (imag, -real)
        else:
            angle = direction * 2.0 * math.pi * index / count
            turn_real, turn_imag = math.cos(angle), math.sin(angle)
            real, imag = (
                real * turn_real - imag * turn_imag,
                real * turn_imag + imag * turn_real,
            )
        base_real, base_imag = even[index]
        first.append((base_real + real, base_imag + imag))
        second.append((base_real - real, base_imag - imag))
    return first + second


def split_dot(table_high, table_low, value):
    high = value.astype(jnp.bfloat16)
    low = (value - high.astype(jnp.float32)).astype(jnp.bfloat16)
    dot = functools.partial(jnp.dot, preferred_element_type=jnp.float32)
    return dot(table_high, high) + (dot(table_high, low) + dot(table_low, high))


def section_kernel(
    total,
    which_ref,
    span_ref,
    value_own,
    value_other,
    slope_own,
    slope_other,
    flow_ref,
    inverse_high,
    inverse_low,
    forward_high,
    forward_low,
    kept_ref,
    sent_ref,
    fields,
    spectra,
):
    short = total // lane_width
    lanes = lane_width
    first = which_ref[0] == 0
    span_wave = span_ref[0]

    def waves_at(residue):
        index = lax.broadcasted_iota(jnp.int32, (lanes, lanes), 0) * short + residue
        return jnp.where(index < total // 2, index, index - total)

    @pl.loop(0, short)
    def _(residue):
        rows = pl.ds(residue, lanes, stride=short)
        own, other = value_own[rows, :], value_other[rows, :]
        value_real, value_imag = jnp.where(first, own, other), jnp.where(first, other, own)
        own, other = slope_own[rows, :], slope_other[rows, :]
        slope_real, slope_imag = jnp.where(first, own, other), jnp.where(first, other, own)
        zonal = waves_at(residue).astype(jnp.float32) * (2.0 * math.pi / total)
        stacked = jnp.concatenate(
            [
                jnp.concatenate([value_real, -zonal * value_imag, slope_real], 1),
                jnp.concatenate([value_imag, zonal * value_real, slope_imag], 1),
            ],
            0,
        )
        fields[residue] = split_dot(inverse_high[residue], inverse_low[residue], stacked)

    background = flow_ref[0, pl.ds(total + which_ref[1], 1), :]

    @pl.loop(0, lanes // 8)
    def _(chunk):
        start = pl.multiple_of(chunk * 8, 8)

        def grid_field(at):
            columns = slice(at * lanes, (at + 1) * lanes)
            return short_transform(
                [
                    (
                        fields[e, pl.ds(start, 8), columns],
                        fields[e, pl.ds(start + lanes, 8), columns],
                    )
                    for e in range(short)
                ],
                1.0,
            )

        def flow(axis, d):
            return flow_ref[axis, pl.ds(start + d * lanes, 8), :]

        advect = []
        for d, (real, imag) in enumerate(grid_field(1)):
            zonal_flow = flow(0, d)
            advect.append((zonal_flow * real, zonal_flow * imag))
        for d, (real, imag) in enumerate(grid_field(0)):
            span_flow = flow(1, d) * span_wave
            advect[d] = (advect[d][0] - span_flow * imag, advect[d][1] + span_flow * real)
        for d, (real, imag) in enumerate(grid_field(2)):
            rise_flow = flow(2, d)
            advect[d] = (
                advect[d][0] + rise_flow * (real + background),
                advect[d][1] + rise_flow * imag,
            )
        for e, (real, imag) in enumerate(short_transform(advect, -1.0)):
            spectra[e, pl.ds(start, 8), :] = real
            spectra[e, pl.ds(start + lanes, 8), :] = imag

    @pl.loop(0, short)
    def _(residue):
        rows = pl.ds(residue, lanes, stride=short)
        result = split_dot(forward_high[residue], forward_low[residue], spectra[residue])
        retained = jnp.abs(waves_at(residue)) <= total // 3
        real = jnp.where(retained, result[:lanes], 0.0)
        imag = jnp.where(retained, result[lanes:], 0.0)
        kept_ref[rows, :] = jnp.where(first, real, imag)
        sent_ref[rows, :] = jnp.where(first, imag, real)


def advance_waves(total, levels, which, span_wave, own, other, flow):
    lanes = lane_width
    blocks = levels // lanes
    short = total // lanes
    tables = [jnp.asarray(table) for table in wide_tables(total)]
    value_spec = pl.BlockSpec((total, lanes), lambda i: (0, i))
    slope_spec = pl.BlockSpec((total, lanes), lambda i: (0, blocks + i))
    table_spec = pl.BlockSpec((short, 2 * lanes, 2 * lanes), lambda i: (0, 0, 0))
    scalars = pl.BlockSpec(memory_space=pltpu.SMEM)
    return pl.pallas_call(
        functools.partial(section_kernel, total),
        grid=(blocks,),
        in_specs=[
            scalars,
            scalars,
            value_spec,
            value_spec,
            slope_spec,
            slope_spec,
            pl.BlockSpec((3, flow.shape[1], lanes), lambda i: (0, 0, i)),
        ]
        + [table_spec] * 4,
        out_specs=[value_spec, value_spec],
        out_shape=[jax.ShapeDtypeStruct((total, levels), jnp.float32)] * 2,
        scratch_shapes=[
            pltpu.VMEM((short, 2 * lanes, 3 * lanes), jnp.float32),
            pltpu.VMEM((short, 2 * lanes, lanes), jnp.float32),
        ],
        compiler_params=pltpu.CompilerParams(vmem_limit_bytes=56 * 1024 * 1024),
    )(which, span_wave, own, other, own, other, flow, *tables)


def by_section(
    coefficients,
    vertical_modes,
    mode_slopes,
    dual_modes,
    eigenvalues,
    velocity,
    gradient,
    span_wavenumbers,
    implicit_rates,
    time_step,
):
    high = lax.Precision.HIGH
    axes = ("row", "col")
    col_count = lax.axis_size("col")
    device_count = lax.axis_size("row") * col_count
    scalars, parts, spans, local_waves, modes = coefficients.shape
    total = local_waves * device_count
    level_count = dual_modes.shape[1]
    half = level_count // 2
    col = lax.axis_index("col")
    device = lax.axis_index("row") * col_count + col
    part, section = device % 2, device // 2
    scalar, span = section // spans, section % spans
    partners = [(at, at ^ 1) for at in range(col_count)]

    pairs = col_count // 2
    level_rows = velocity.shape[1]
    marks = jnp.pad(
        jnp.transpose(gradient)[None], ((0, 2), (0, 0), (0, lane_width - scalars))
    )
    flow = jnp.concatenate([velocity, marks], 2)
    flow = lax.ppermute(
        flow, "col", [(at, 2 * (at % pairs) + at // pairs) for at in range(col_count)]
    )
    groups = [list(range(0, col_count, 2)), list(range(1, col_count, 2))]
    flow = lax.all_gather(flow, "col", axis_index_groups=groups)
    flow = jnp.transpose(flow, (1, 3, 0, 2)).reshape(3, total + lane_width, pairs * level_rows)

    sent = jnp.swapaxes(coefficients, 1, 2).reshape(device_count, local_waves, modes)
    lines = lax.all_to_all(sent, axes, 0, 0, tiled=True).reshape(total, modes)

    def half_of(table, which, axis):
        return lax.dynamic_slice_in_dim(table, which * half, half, axis)

    def to_levels(which):
        table = jnp.concatenate(
            [half_of(vertical_modes, which, 0), half_of(mode_slopes, which, 0)], 0
        )
        return jnp.einsum("pj,zj->pz", lines, table, precision=high)

    other = lax.ppermute(to_levels(1 - part), "col", partners)
    own = to_levels(part)
    which = jnp.stack([part, scalar]).astype(jnp.int32)
    kept, passed = advance_waves(
        total, half, which, span_wavenumbers[span][None], own, other, flow
    )
    received = lax.ppermute(passed, "col", partners)
    forcing = jnp.einsum(
        "pz,jz->pj", kept, half_of(dual_modes, part, 1), precision=high
    ) + jnp.einsum("pz,jz->pj", received, half_of(dual_modes, 1 - part, 1), precision=high)
    forcing = lax.all_to_all(
        forcing.reshape(device_count, local_waves, modes), axes, 0, 0, tiled=True
    )
    forcing = jnp.swapaxes(
        forcing.reshape(scalars, spans, parts, local_waves, modes), 1, 2
    )
    zonal_waves = signed_waves(total).astype(jnp.float32) * (2.0 * math.pi / total)
    own_waves = lax.dynamic_slice_in_dim(zonal_waves, device * local_waves, local_waves)
    denominator = 1.0 + implicit_rates[:, None, None, None, None] * (
        eigenvalues[None, None, None, None, :]
        + own_waves[None, None, None, :, None] ** 2
        + span_wavenumbers[None, None, :, None, None] ** 2
    )
    return (coefficients - time_step * forcing) / denominator


def program(*arrays):
    coefficients, levels = arrays[0], arrays[3].shape[1]
    col_count = lax.axis_size("col")
    device_count = lax.axis_size("row") * col_count
    scalars, _, spans, _, _ = coefficients.shape
    fits = (
        device_count == 2 * scalars * spans
        and col_count % 2 == 0
        and (levels // 2) % lane_width == 0
        and coefficients.shape[3] * device_count == 16 * lane_width
    )
    return by_section(*arrays) if fits else on_device(*arrays)


def solution(mesh):
    in_specs = (
        P(None, None, None, ("row", "col"), None),
        P(),
        P(),
        P(),
        P(),
        P(None, "col", None),
        P(None, "col"),
        P(),
        P(),
        P(),
    )
    out_specs = P(None, None, None, ("row", "col"), None)
    return jax.shard_map(
        program, mesh=mesh, in_specs=in_specs, out_specs=out_specs, check_vma=False
    )
```

```python
import functools
import math

import jax
import jax.numpy as jnp
import ml_dtypes
import numpy as np
from jax import lax
from jax.experimental import pallas as pl
from jax.experimental.pallas import tpu as pltpu
from jax.sharding import PartitionSpec as P

highest = lax.Precision.HIGHEST
lane_width = 128


def signed_waves(length):
    indices = jnp.arange(length, dtype=jnp.int32)
    return jnp.where(indices < length // 2, indices, indices - length)


def phase_table(row_total, col_total, period, direction):
    left_index = jnp.arange(row_total, dtype=jnp.int32)[:, None]
    right_index = jnp.arange(col_total, dtype=jnp.int32)[None, :]
    angles = (left_index * right_index % period).astype(jnp.float32) * (2.0 * math.pi / period)
    return (jnp.cos(angles), direction * jnp.sin(angles))


def contract(form, left_real, left_imag, right_real, right_imag):
    product_real = jnp.einsum(form, left_real, right_real, precision=highest) - jnp.einsum(
        form, left_imag, right_imag, precision=highest
    )
    product_imag = jnp.einsum(form, left_real, right_imag, precision=highest) + jnp.einsum(
        form, left_imag, right_real, precision=highest
    )
    return (product_real, product_imag)


def twisted(real_in, imag_in, twist_real, twist_imag):
    return (
        real_in * twist_real - imag_in * twist_imag,
        real_in * twist_imag + imag_in * twist_real,
    )


def inverse_transform(real_in, imag_in, length):
    short_size = length // lane_width
    scale = 1.0 / math.sqrt(length)
    short_real, short_imag = phase_table(short_size, short_size, short_size, 1.0)
    twist_real, twist_imag = phase_table(short_size, lane_width, length, 1.0)
    wide_real, wide_imag = phase_table(lane_width, lane_width, lane_width, 1.0)
    middle_real, middle_imag = contract("...ef,ed->...df", real_in, imag_in, short_real, short_imag)
    middle_real, middle_imag = twisted(middle_real, middle_imag, twist_real, twist_imag)
    return contract(
        "...df,fc->...dc", middle_real, middle_imag, wide_real * scale, wide_imag * scale
    )


def forward_transform(real_in, imag_in, length):
    short_size = length // lane_width
    scale = 1.0 / math.sqrt(length)
    short_real, short_imag = phase_table(short_size, short_size, short_size, -1.0)
    twist_real, twist_imag = phase_table(short_size, lane_width, length, -1.0)
    wide_real, wide_imag = phase_table(lane_width, lane_width, lane_width, -1.0)
    middle_real, middle_imag = contract("...dc,cf->...df", real_in, imag_in, wide_real, wide_imag)
    middle_real, middle_imag = twisted(middle_real, middle_imag, twist_real, twist_imag)
    return contract(
        "...df,de->...ef", middle_real, middle_imag, short_real * scale, short_imag * scale
    )


def on_device(
    coefficients,
    vertical_modes,
    mode_slopes,
    dual_modes,
    eigenvalues,
    velocity,
    gradient,
    span_wavenumbers,
    implicit_rates,
    time_step,
):
    row_count = lax.axis_size("row")
    col_count = lax.axis_size("col")
    local_waves = coefficients.shape[3]
    total_points = local_waves * row_count * col_count
    short_size = total_points // lane_width
    first_wave = (lax.axis_index("row") * col_count + lax.axis_index("col")) * local_waves
    signed = signed_waves(total_points)
    zonal_waves = signed.astype(jnp.float32) * (2.0 * math.pi / total_points)
    own_waves = lax.dynamic_slice_in_dim(zonal_waves, first_wave, local_waves)
    value_real = jnp.einsum("sqpj,zj->zsqp", coefficients[:, 0], vertical_modes, precision=highest)
    value_imag = jnp.einsum("sqpj,zj->zsqp", coefficients[:, 1], vertical_modes, precision=highest)
    slope_real = jnp.einsum("sqpj,zj->zsqp", coefficients[:, 0], mode_slopes, precision=highest)
    slope_imag = jnp.einsum("sqpj,zj->zsqp", coefficients[:, 1], mode_slopes, precision=highest)
    fields = (
        lax.all_to_all(value_real, "col", split_axis=0, concat_axis=3, tiled=True),
        lax.all_to_all(value_imag, "col", split_axis=0, concat_axis=3, tiled=True),
        lax.all_to_all(slope_real, "col", split_axis=0, concat_axis=3, tiled=True),
        lax.all_to_all(slope_imag, "col", split_axis=0, concat_axis=3, tiled=True),
    )
    fields = (
        lax.all_to_all(fields[0], "row", split_axis=2, concat_axis=3, tiled=True),
        lax.all_to_all(fields[1], "row", split_axis=2, concat_axis=3, tiled=True),
        lax.all_to_all(fields[2], "row", split_axis=2, concat_axis=3, tiled=True),
        lax.all_to_all(fields[3], "row", split_axis=2, concat_axis=3, tiled=True),
    )
    level_rows = fields[0].shape[0]
    span_rows = fields[0].shape[2]
    grid_shape = (level_rows, 2, span_rows, short_size, lane_width)
    value_real = fields[0].reshape(grid_shape)
    value_imag = fields[1].reshape(grid_shape)
    slope_real = fields[2].reshape(grid_shape)
    slope_imag = fields[3].reshape(grid_shape)
    wave_grid = zonal_waves.reshape(short_size, lane_width)
    scalar_real, scalar_imag = inverse_transform(value_real, value_imag, total_points)
    zonal_real, zonal_imag = inverse_transform(
        -wave_grid * value_imag, wave_grid * value_real, total_points
    )
    rise_real, rise_imag = inverse_transform(slope_real, slope_imag, total_points)
    flow = jnp.swapaxes(velocity.reshape(3, level_rows, lane_width, short_size), -1, -2)
    zonal_flow = flow[0][:, None, None]
    span_flow = flow[1][:, None, None]
    rise_flow = flow[2][:, None, None]
    span_waves = lax.dynamic_slice_in_dim(
        span_wavenumbers, lax.axis_index("row") * span_rows, span_rows
    )[None, None, :, None, None]
    background = jnp.transpose(gradient)[:, :, None, None, None]
    advect_real = (
        zonal_flow * zonal_real
        - span_waves * span_flow * scalar_imag
        + rise_flow * rise_real
        + rise_flow * background
    )
    advect_imag = (
        zonal_flow * zonal_imag + span_waves * span_flow * scalar_real + rise_flow * rise_imag
    )
    spectra_real, spectra_imag = forward_transform(advect_real, advect_imag, total_points)
    retained = (
        (jnp.abs(signed) <= total_points // 3).astype(jnp.float32).reshape(short_size, lane_width)
    )
    flat_shape = (level_rows, 2, span_rows, total_points)
    spectra_real = (spectra_real * retained).reshape(flat_shape)
    spectra_imag = (spectra_imag * retained).reshape(flat_shape)
    returned_real, returned_imag = (
        lax.all_to_all(
            lax.all_to_all(spectra_real, "row", split_axis=3, concat_axis=2, tiled=True),
            "col",
            split_axis=3,
            concat_axis=0,
            tiled=True,
        ),
        lax.all_to_all(
            lax.all_to_all(spectra_imag, "row", split_axis=3, concat_axis=2, tiled=True),
            "col",
            split_axis=3,
            concat_axis=0,
            tiled=True,
        ),
    )
    forcing_real = jnp.einsum("zsqp,jz->sqpj", returned_real, dual_modes, precision=highest)
    forcing_imag = jnp.einsum("zsqp,jz->sqpj", returned_imag, dual_modes, precision=highest)
    forcing = jnp.stack([forcing_real, forcing_imag], 1)
    denominator = 1.0 + implicit_rates[:, None, None, None, None] * (
        eigenvalues[None, None, None, None, :]
        + own_waves[None, None, None, :, None] ** 2
        + span_wavenumbers[None, None, :, None, None] ** 2
    )
    return (coefficients - time_step * forcing) / denominator


def wide_tables(total):
    short = total // lane_width
    points = np.arange(lane_width)[None, :, None]
    waves = np.arange(lane_width)[None, None, :] * short + np.arange(short)[:, None, None]
    angles = (points * waves % total) * (2.0 * math.pi / total)
    scale = 1.0 / math.sqrt(total)
    cosines, sines = np.cos(angles) * scale, np.sin(angles) * scale
    inverse = np.concatenate(
        [
            np.concatenate([cosines, -sines], 2),
            np.concatenate([sines, cosines], 2),
        ],
        1,
    )
    tables = []
    for table in (inverse, np.swapaxes(inverse, 1, 2)):
        high = table.astype(ml_dtypes.bfloat16)
        low = (table - high.astype(np.float64)).astype(ml_dtypes.bfloat16)
        tables += [high, low]
    return tables


def short_transform(values, direction):
    count = len(values)
    if count == 1:
        return values
    even = short_transform(values[0::2], direction)
    odd = short_transform(values[1::2], direction)
    first, second = [], []
    for index in range(count // 2):
        real, imag = odd[index]
        if index == 0:
            pass
        elif 4 * index == count:
            real, imag = (-imag, real) if direction > 0 else (imag, -real)
        else:
            angle = direction * 2.0 * math.pi * index / count
            turn_real, turn_imag = math.cos(angle), math.sin(angle)
            real, imag = (
                real * turn_real - imag * turn_imag,
                real * turn_imag + imag * turn_real,
            )
        base_real, base_imag = even[index]
        first.append((base_real + real, base_imag + imag))
        second.append((base_real - real, base_imag - imag))
    return first + second


def split_dot(table_high, table_low, value):
    high = value.astype(jnp.bfloat16)
    low = (value - high.astype(jnp.float32)).astype(jnp.bfloat16)
    dot = functools.partial(jnp.dot, preferred_element_type=jnp.float32)
    return dot(table_high, high) + (dot(table_high, low) + dot(table_low, high))


def section_kernel(
    total,
    which_ref,
    span_ref,
    value_own,
    value_other,
    slope_own,
    slope_other,
    flow_ref,
    inverse_high,
    inverse_low,
    forward_high,
    forward_low,
    kept_ref,
    sent_ref,
    fields,
    spectra,
):
    short = total // lane_width
    lanes = lane_width
    first = which_ref[0] == 0
    span_wave = span_ref[0]

    def waves_at(residue):
        index = lax.broadcasted_iota(jnp.int32, (lanes, lanes), 0) * short + residue
        return jnp.where(index < total // 2, index, index - total)

    @pl.loop(0, short)
    def _(residue):
        rows = pl.ds(residue, lanes, stride=short)
        own, other = value_own[rows, :], value_other[rows, :]
        value_real, value_imag = jnp.where(first, own, other), jnp.where(first, other, own)
        own, other = slope_own[rows, :], slope_other[rows, :]
        slope_real, slope_imag = jnp.where(first, own, other), jnp.where(first, other, own)
        zonal = waves_at(residue).astype(jnp.float32) * (2.0 * math.pi / total)
        stacked = jnp.concatenate(
            [
                jnp.concatenate([value_real, -zonal * value_imag, slope_real], 1),
                jnp.concatenate([value_imag, zonal * value_real, slope_imag], 1),
            ],
            0,
        )
        fields[residue] = split_dot(inverse_high[residue], inverse_low[residue], stacked)

    background = flow_ref[0, pl.ds(total + which_ref[1], 1), :]

    @pl.loop(0, lanes // 8)
    def _(chunk):
        start = pl.multiple_of(chunk * 8, 8)

        def grid_field(at):
            columns = slice(at * lanes, (at + 1) * lanes)
            return short_transform(
                [
                    (
                        fields[e, pl.ds(start, 8), columns],
                        fields[e, pl.ds(start + lanes, 8), columns],
                    )
                    for e in range(short)
                ],
                1.0,
            )

        def flow(axis, d):
            return flow_ref[axis, pl.ds(start + d * lanes, 8), :]

        advect = []
        for d, (real, imag) in enumerate(grid_field(1)):
            zonal_flow = flow(0, d)
            advect.append((zonal_flow * real, zonal_flow * imag))
        for d, (real, imag) in enumerate(grid_field(0)):
            span_flow = flow(1, d) * span_wave
            advect[d] = (advect[d][0] - span_flow * imag, advect[d][1] + span_flow * real)
        for d, (real, imag) in enumerate(grid_field(2)):
            rise_flow = flow(2, d)
            advect[d] = (
                advect[d][0] + rise_flow * (real + background),
                advect[d][1] + rise_flow * imag,
            )
        for e, (real, imag) in enumerate(short_transform(advect, -1.0)):
            spectra[e, pl.ds(start, 8), :] = real
            spectra[e, pl.ds(start + lanes, 8), :] = imag

    @pl.loop(0, short)
    def _(residue):
        rows = pl.ds(residue, lanes, stride=short)
        result = split_dot(forward_high[residue], forward_low[residue], spectra[residue])
        retained = jnp.abs(waves_at(residue)) <= total // 3
        real = jnp.where(retained, result[:lanes], 0.0)
        imag = jnp.where(retained, result[lanes:], 0.0)
        kept_ref[rows, :] = jnp.where(first, real, imag)
        sent_ref[rows, :] = jnp.where(first, imag, real)


def advance_waves(total, levels, which, span_wave, own, other, flow):
    lanes = lane_width
    blocks = levels // lanes
    short = total // lanes
    tables = [jnp.asarray(table) for table in wide_tables(total)]
    value_spec = pl.BlockSpec((total, lanes), lambda i: (0, i))
    slope_spec = pl.BlockSpec((total, lanes), lambda i: (0, blocks + i))
    table_spec = pl.BlockSpec((short, 2 * lanes, 2 * lanes), lambda i: (0, 0, 0))
    scalars = pl.BlockSpec(memory_space=pltpu.SMEM)
    return pl.pallas_call(
        functools.partial(section_kernel, total),
        grid=(blocks,),
        in_specs=[
            scalars,
            scalars,
            value_spec,
            value_spec,
            slope_spec,
            slope_spec,
            pl.BlockSpec((3, flow.shape[1], lanes), lambda i: (0, 0, i)),
        ]
        + [table_spec] * 4,
        out_specs=[value_spec, value_spec],
        out_shape=[jax.ShapeDtypeStruct((total, levels), jnp.float32)] * 2,
        scratch_shapes=[
            pltpu.VMEM((short, 2 * lanes, 3 * lanes), jnp.float32),
            pltpu.VMEM((short, 2 * lanes, lanes), jnp.float32),
        ],
        compiler_params=pltpu.CompilerParams(vmem_limit_bytes=56 * 1024 * 1024),
    )(which, span_wave, own, other, own, other, flow, *tables)


def by_section(
    coefficients,
    vertical_modes,
    mode_slopes,
    dual_modes,
    eigenvalues,
    velocity,
    gradient,
    span_wavenumbers,
    implicit_rates,
    time_step,
):
    high = lax.Precision.HIGH
    axes = ("row", "col")
    col_count = lax.axis_size("col")
    device_count = lax.axis_size("row") * col_count
    scalars, parts, spans, local_waves, modes = coefficients.shape
    total = local_waves * device_count
    level_count = dual_modes.shape[1]
    half = level_count // 2
    col = lax.axis_index("col")
    device = lax.axis_index("row") * col_count + col
    part, section = device % 2, device // 2
    scalar, span = section // spans, section % spans
    partners = [(at, at ^ 1) for at in range(col_count)]

    pairs = col_count // 2
    level_rows = velocity.shape[1]
    marks = jnp.pad(
        jnp.transpose(gradient)[None], ((0, 2), (0, 0), (0, lane_width - scalars))
    )
    flow = jnp.concatenate([velocity, marks], 2)
    groups = [list(range(0, col_count, 2)), list(range(1, col_count, 2))]
    flow = lax.all_gather(flow, "col", axis_index_groups=groups)
    flow = jnp.transpose(flow, (1, 3, 0, 2)).reshape(3, total + lane_width, pairs * level_rows)

    sent = jnp.swapaxes(coefficients, 1, 2).reshape(device_count, local_waves, modes)
    lines = lax.all_to_all(sent, axes, 0, 0, tiled=True).reshape(total, modes)

    def half_of(table, which, axis):
        shape = table.shape[:axis] + (pairs, 2, level_rows) + table.shape[axis + 1 :]
        taken = lax.dynamic_index_in_dim(table.reshape(shape), which, axis + 1, keepdims=False)
        return taken.reshape(table.shape[:axis] + (half,) + table.shape[axis + 1 :])

    def to_levels(which):
        table = jnp.concatenate(
            [half_of(vertical_modes, which, 0), half_of(mode_slopes, which, 0)], 0
        )
        return jnp.einsum("pj,zj->pz", lines, table, precision=high)

    other = lax.ppermute(to_levels(1 - part), "col", partners)
    own = to_levels(part)
    which = jnp.stack([part, scalar]).astype(jnp.int32)
    kept, passed = advance_waves(
        total, half, which, span_wavenumbers[span][None], own, other, flow
    )
    received = lax.ppermute(passed, "col", partners)
    forcing = jnp.einsum(
        "pz,jz->pj", kept, half_of(dual_modes, part, 1), precision=high
    ) + jnp.einsum("pz,jz->pj", received, half_of(dual_modes, 1 - part, 1), precision=high)
    forcing = lax.all_to_all(
        forcing.reshape(device_count, local_waves, modes), axes, 0, 0, tiled=True
    )
    forcing = jnp.swapaxes(
        forcing.reshape(scalars, spans, parts, local_waves, modes), 1, 2
    )
    zonal_waves = signed_waves(total).astype(jnp.float32) * (2.0 * math.pi / total)
    own_waves = lax.dynamic_slice_in_dim(zonal_waves, device * local_waves, local_waves)
    denominator = 1.0 + implicit_rates[:, None, None, None, None] * (
        eigenvalues[None, None, None, None, :]
        + own_waves[None, None, None, :, None] ** 2
        + span_wavenumbers[None, None, :, None, None] ** 2
    )
    return (coefficients - time_step * forcing) / denominator


def program(*arrays):
    coefficients, levels = arrays[0], arrays[3].shape[1]
    col_count = lax.axis_size("col")
    device_count = lax.axis_size("row") * col_count
    scalars, _, spans, _, _ = coefficients.shape
    fits = (
        device_count == 2 * scalars * spans
        and col_count % 2 == 0
        and (levels // 2) % lane_width == 0
        and coefficients.shape[3] * device_count == 16 * lane_width
    )
    return by_section(*arrays) if fits else on_device(*arrays)


def solution(mesh):
    in_specs = (
        P(None, None, None, ("row", "col"), None),
        P(),
        P(),
        P(),
        P(),
        P(None, "col", None),
        P(None, "col"),
        P(),
        P(),
        P(),
    )
    out_specs = P(None, None, None, ("row", "col"), None)
    return jax.shard_map(
        program, mesh=mesh, in_specs=in_specs, out_specs=out_specs, check_vma=False
    )
```

```python
import functools
import math

import jax
import jax.numpy as jnp
import ml_dtypes
import numpy as np
from jax import lax
from jax.experimental import pallas as pl
from jax.experimental.pallas import tpu as pltpu
from jax.sharding import PartitionSpec as P

highest = lax.Precision.HIGHEST
lane_width = 128


def signed_waves(length):
    indices = jnp.arange(length, dtype=jnp.int32)
    return jnp.where(indices < length // 2, indices, indices - length)


def phase_table(row_total, col_total, period, direction):
    left_index = jnp.arange(row_total, dtype=jnp.int32)[:, None]
    right_index = jnp.arange(col_total, dtype=jnp.int32)[None, :]
    angles = (left_index * right_index % period).astype(jnp.float32) * (2.0 * math.pi / period)
    return (jnp.cos(angles), direction * jnp.sin(angles))


def contract(form, left_real, left_imag, right_real, right_imag):
    product_real = jnp.einsum(form, left_real, right_real, precision=highest) - jnp.einsum(
        form, left_imag, right_imag, precision=highest
    )
    product_imag = jnp.einsum(form, left_real, right_imag, precision=highest) + jnp.einsum(
        form, left_imag, right_real, precision=highest
    )
    return (product_real, product_imag)


def twisted(real_in, imag_in, twist_real, twist_imag):
    return (
        real_in * twist_real - imag_in * twist_imag,
        real_in * twist_imag + imag_in * twist_real,
    )


def inverse_transform(real_in, imag_in, length):
    short_size = length // lane_width
    scale = 1.0 / math.sqrt(length)
    short_real, short_imag = phase_table(short_size, short_size, short_size, 1.0)
    twist_real, twist_imag = phase_table(short_size, lane_width, length, 1.0)
    wide_real, wide_imag = phase_table(lane_width, lane_width, lane_width, 1.0)
    middle_real, middle_imag = contract("...ef,ed->...df", real_in, imag_in, short_real, short_imag)
    middle_real, middle_imag = twisted(middle_real, middle_imag, twist_real, twist_imag)
    return contract(
        "...df,fc->...dc", middle_real, middle_imag, wide_real * scale, wide_imag * scale
    )


def forward_transform(real_in, imag_in, length):
    short_size = length // lane_width
    scale = 1.0 / math.sqrt(length)
    short_real, short_imag = phase_table(short_size, short_size, short_size, -1.0)
    twist_real, twist_imag = phase_table(short_size, lane_width, length, -1.0)
    wide_real, wide_imag = phase_table(lane_width, lane_width, lane_width, -1.0)
    middle_real, middle_imag = contract("...dc,cf->...df", real_in, imag_in, wide_real, wide_imag)
    middle_real, middle_imag = twisted(middle_real, middle_imag, twist_real, twist_imag)
    return contract(
        "...df,de->...ef", middle_real, middle_imag, short_real * scale, short_imag * scale
    )


def on_device(
    coefficients,
    vertical_modes,
    mode_slopes,
    dual_modes,
    eigenvalues,
    velocity,
    gradient,
    span_wavenumbers,
    implicit_rates,
    time_step,
):
    row_count = lax.axis_size("row")
    col_count = lax.axis_size("col")
    local_waves = coefficients.shape[3]
    total_points = local_waves * row_count * col_count
    short_size = total_points // lane_width
    first_wave = (lax.axis_index("row") * col_count + lax.axis_index("col")) * local_waves
    signed = signed_waves(total_points)
    zonal_waves = signed.astype(jnp.float32) * (2.0 * math.pi / total_points)
    own_waves = lax.dynamic_slice_in_dim(zonal_waves, first_wave, local_waves)
    value_real = jnp.einsum("sqpj,zj->zsqp", coefficients[:, 0], vertical_modes, precision=highest)
    value_imag = jnp.einsum("sqpj,zj->zsqp", coefficients[:, 1], vertical_modes, precision=highest)
    slope_real = jnp.einsum("sqpj,zj->zsqp", coefficients[:, 0], mode_slopes, precision=highest)
    slope_imag = jnp.einsum("sqpj,zj->zsqp", coefficients[:, 1], mode_slopes, precision=highest)
    fields = (
        lax.all_to_all(value_real, "col", split_axis=0, concat_axis=3, tiled=True),
        lax.all_to_all(value_imag, "col", split_axis=0, concat_axis=3, tiled=True),
        lax.all_to_all(slope_real, "col", split_axis=0, concat_axis=3, tiled=True),
        lax.all_to_all(slope_imag, "col", split_axis=0, concat_axis=3, tiled=True),
    )
    fields = (
        lax.all_to_all(fields[0], "row", split_axis=2, concat_axis=3, tiled=True),
        lax.all_to_all(fields[1], "row", split_axis=2, concat_axis=3, tiled=True),
        lax.all_to_all(fields[2], "row", split_axis=2, concat_axis=3, tiled=True),
        lax.all_to_all(fields[3], "row", split_axis=2, concat_axis=3, tiled=True),
    )
    level_rows = fields[0].shape[0]
    span_rows = fields[0].shape[2]
    grid_shape = (level_rows, 2, span_rows, short_size, lane_width)
    value_real = fields[0].reshape(grid_shape)
    value_imag = fields[1].reshape(grid_shape)
    slope_real = fields[2].reshape(grid_shape)
    slope_imag = fields[3].reshape(grid_shape)
    wave_grid = zonal_waves.reshape(short_size, lane_width)
    scalar_real, scalar_imag = inverse_transform(value_real, value_imag, total_points)
    zonal_real, zonal_imag = inverse_transform(
        -wave_grid * value_imag, wave_grid * value_real, total_points
    )
    rise_real, rise_imag = inverse_transform(slope_real, slope_imag, total_points)
    flow = jnp.swapaxes(velocity.reshape(3, level_rows, lane_width, short_size), -1, -2)
    zonal_flow = flow[0][:, None, None]
    span_flow = flow[1][:, None, None]
    rise_flow = flow[2][:, None, None]
    span_waves = lax.dynamic_slice_in_dim(
        span_wavenumbers, lax.axis_index("row") * span_rows, span_rows
    )[None, None, :, None, None]
    background = jnp.transpose(gradient)[:, :, None, None, None]
    advect_real = (
        zonal_flow * zonal_real
        - span_waves * span_flow * scalar_imag
        + rise_flow * rise_real
        + rise_flow * background
    )
    advect_imag = (
        zonal_flow * zonal_imag + span_waves * span_flow * scalar_real + rise_flow * rise_imag
    )
    spectra_real, spectra_imag = forward_transform(advect_real, advect_imag, total_points)
    retained = (
        (jnp.abs(signed) <= total_points // 3).astype(jnp.float32).reshape(short_size, lane_width)
    )
    flat_shape = (level_rows, 2, span_rows, total_points)
    spectra_real = (spectra_real * retained).reshape(flat_shape)
    spectra_imag = (spectra_imag * retained).reshape(flat_shape)
    returned_real, returned_imag = (
        lax.all_to_all(
            lax.all_to_all(spectra_real, "row", split_axis=3, concat_axis=2, tiled=True),
            "col",
            split_axis=3,
            concat_axis=0,
            tiled=True,
        ),
        lax.all_to_all(
            lax.all_to_all(spectra_imag, "row", split_axis=3, concat_axis=2, tiled=True),
            "col",
            split_axis=3,
            concat_axis=0,
            tiled=True,
        ),
    )
    forcing_real = jnp.einsum("zsqp,jz->sqpj", returned_real, dual_modes, precision=highest)
    forcing_imag = jnp.einsum("zsqp,jz->sqpj", returned_imag, dual_modes, precision=highest)
    forcing = jnp.stack([forcing_real, forcing_imag], 1)
    denominator = 1.0 + implicit_rates[:, None, None, None, None] * (
        eigenvalues[None, None, None, None, :]
        + own_waves[None, None, None, :, None] ** 2
        + span_wavenumbers[None, None, :, None, None] ** 2
    )
    return (coefficients - time_step * forcing) / denominator


def wide_tables(total):
    short = total // lane_width
    points = np.arange(lane_width)[None, :, None]
    waves = np.arange(lane_width)[None, None, :] * short + np.arange(short)[:, None, None]
    angles = (points * waves % total) * (2.0 * math.pi / total)
    scale = 1.0 / math.sqrt(total)
    cosines, sines = np.cos(angles) * scale, np.sin(angles) * scale
    inverse = np.concatenate(
        [
            np.concatenate([cosines, -sines], 2),
            np.concatenate([sines, cosines], 2),
        ],
        1,
    )
    tables = []
    for table in (inverse, np.swapaxes(inverse, 1, 2)):
        high = table.astype(ml_dtypes.bfloat16)
        low = (table - high.astype(np.float64)).astype(ml_dtypes.bfloat16)
        tables += [high, low]
    return tables


def short_transform(values, direction):
    count = len(values)
    if count == 1:
        return values
    even = short_transform(values[0::2], direction)
    odd = short_transform(values[1::2], direction)
    first, second = [], []
    for index in range(count // 2):
        real, imag = odd[index]
        if index == 0:
            pass
        elif 4 * index == count:
            real, imag = (-imag, real) if direction > 0 else (imag, -real)
        else:
            angle = direction * 2.0 * math.pi * index / count
            turn_real, turn_imag = math.cos(angle), math.sin(angle)
            real, imag = (
                real * turn_real - imag * turn_imag,
                real * turn_imag + imag * turn_real,
            )
        base_real, base_imag = even[index]
        first.append((base_real + real, base_imag + imag))
        second.append((base_real - real, base_imag - imag))
    return first + second


def split_dot(table_high, table_low, value):
    high = value.astype(jnp.bfloat16)
    low = (value - high.astype(jnp.float32)).astype(jnp.bfloat16)
    dot = functools.partial(jnp.dot, preferred_element_type=jnp.float32)
    return dot(table_high, high) + (dot(table_high, low) + dot(table_low, high))


def section_kernel(
    total,
    which_ref,
    span_ref,
    value_own,
    value_other,
    slope_own,
    slope_other,
    flow_ref,
    inverse_high,
    inverse_low,
    forward_high,
    forward_low,
    kept_ref,
    sent_ref,
    fields,
    spectra,
):
    short = total // lane_width
    lanes = lane_width
    first = which_ref[0] == 0
    span_wave = span_ref[0]

    def waves_at(residue):
        index = lax.broadcasted_iota(jnp.int32, (lanes, lanes), 0) * short + residue
        return jnp.where(index < total // 2, index, index - total)

    @pl.loop(0, short)
    def _(residue):
        rows = pl.ds(residue, lanes, stride=short)
        own, other = value_own[rows, :], value_other[rows, :]
        value_real, value_imag = jnp.where(first, own, other), jnp.where(first, other, own)
        own, other = slope_own[rows, :], slope_other[rows, :]
        slope_real, slope_imag = jnp.where(first, own, other), jnp.where(first, other, own)
        zonal = waves_at(residue).astype(jnp.float32) * (2.0 * math.pi / total)
        stacked = jnp.concatenate(
            [
                jnp.concatenate([value_real, -zonal * value_imag, slope_real], 1),
                jnp.concatenate([value_imag, zonal * value_real, slope_imag], 1),
            ],
            0,
        )
        fields[residue] = split_dot(inverse_high[residue], inverse_low[residue], stacked)

    background = flow_ref[0, pl.ds(total + which_ref[1], 1), :]

    @pl.loop(0, lanes // 8)
    def _(chunk):
        start = pl.multiple_of(chunk * 8, 8)

        def grid_field(at):
            columns = slice(at * lanes, (at + 1) * lanes)
            return short_transform(
                [
                    (
                        fields[e, pl.ds(start, 8), columns],
                        fields[e, pl.ds(start + lanes, 8), columns],
                    )
                    for e in range(short)
                ],
                1.0,
            )

        def flow(axis, d):
            return flow_ref[axis, pl.ds(start + d * lanes, 8), :]

        advect = []
        for d, (real, imag) in enumerate(grid_field(1)):
            zonal_flow = flow(0, d)
            advect.append((zonal_flow * real, zonal_flow * imag))
        for d, (real, imag) in enumerate(grid_field(0)):
            span_flow = flow(1, d) * span_wave
            advect[d] = (advect[d][0] - span_flow * imag, advect[d][1] + span_flow * real)
        for d, (real, imag) in enumerate(grid_field(2)):
            rise_flow = flow(2, d)
            advect[d] = (
                advect[d][0] + rise_flow * (real + background),
                advect[d][1] + rise_flow * imag,
            )
        for e, (real, imag) in enumerate(short_transform(advect, -1.0)):
            spectra[e, pl.ds(start, 8), :] = real
            spectra[e, pl.ds(start + lanes, 8), :] = imag

    @pl.loop(0, short)
    def _(residue):
        rows = pl.ds(residue, lanes, stride=short)
        result = split_dot(forward_high[residue], forward_low[residue], spectra[residue])
        retained = jnp.abs(waves_at(residue)) <= total // 3
        real = jnp.where(retained, result[:lanes], 0.0)
        imag = jnp.where(retained, result[lanes:], 0.0)
        kept_ref[rows, :] = jnp.where(first, real, imag)
        sent_ref[rows, :] = jnp.where(first, imag, real)


def advance_waves(total, levels, which, span_wave, own, other, flow):
    lanes = lane_width
    blocks = levels // lanes
    short = total // lanes
    tables = [jnp.asarray(table) for table in wide_tables(total)]
    value_spec = pl.BlockSpec((total, lanes), lambda i: (0, i))
    slope_spec = pl.BlockSpec((total, lanes), lambda i: (0, blocks + i))
    table_spec = pl.BlockSpec((short, 2 * lanes, 2 * lanes), lambda i: (0, 0, 0))
    scalars = pl.BlockSpec(memory_space=pltpu.SMEM)
    return pl.pallas_call(
        functools.partial(section_kernel, total),
        grid=(blocks,),
        in_specs=[
            scalars,
            scalars,
            value_spec,
            value_spec,
            slope_spec,
            slope_spec,
            pl.BlockSpec((3, flow.shape[1], lanes), lambda i: (0, 0, i)),
        ]
        + [table_spec] * 4,
        out_specs=[value_spec, value_spec],
        out_shape=[jax.ShapeDtypeStruct((total, levels), jnp.float32)] * 2,
        scratch_shapes=[
            pltpu.VMEM((short, 2 * lanes, 3 * lanes), jnp.float32),
            pltpu.VMEM((short, 2 * lanes, lanes), jnp.float32),
        ],
        compiler_params=pltpu.CompilerParams(vmem_limit_bytes=56 * 1024 * 1024),
    )(which, span_wave, own, other, own, other, flow, *tables)


def by_section(
    coefficients,
    vertical_modes,
    mode_slopes,
    dual_modes,
    eigenvalues,
    velocity,
    gradient,
    span_wavenumbers,
    implicit_rates,
    time_step,
):
    high = lax.Precision.HIGH
    axes = ("row", "col")
    col_count = lax.axis_size("col")
    device_count = lax.axis_size("row") * col_count
    scalars, parts, spans, local_waves, modes = coefficients.shape
    total = local_waves * device_count
    level_count = dual_modes.shape[1]
    half = level_count // 2
    col = lax.axis_index("col")
    device = lax.axis_index("row") * col_count + col
    part, section = device % 2, device // 2
    scalar, span = section // spans, section % spans
    partners = [(at, at ^ 1) for at in range(col_count)]

    pairs = col_count // 2
    level_rows = velocity.shape[1]
    marks = jnp.pad(
        jnp.transpose(gradient)[None], ((0, 2), (0, 0), (0, lane_width - scalars))
    )
    flow = jnp.concatenate([velocity, marks], 2)
    row_count = lax.axis_size("row")
    share = level_rows // row_count
    flow = lax.dynamic_slice_in_dim(flow, lax.axis_index("row") * share, share, 1)
    groups = [list(range(0, device_count, 2)), list(range(1, device_count, 2))]
    flow = lax.all_gather(flow, axes, axis_index_groups=groups)
    flow = flow.reshape(row_count, pairs, 3, share, total + lane_width)
    flow = jnp.transpose(flow, (2, 4, 1, 0, 3)).reshape(3, total + lane_width, half)

    sent = jnp.swapaxes(coefficients, 1, 2).reshape(device_count, local_waves, modes)
    lines = lax.all_to_all(sent, axes, 0, 0, tiled=True).reshape(total, modes)

    def half_of(table, which, axis):
        shape = table.shape[:axis] + (pairs, 2, level_rows) + table.shape[axis + 1 :]
        taken = lax.dynamic_index_in_dim(table.reshape(shape), which, axis + 1, keepdims=False)
        return taken.reshape(table.shape[:axis] + (half,) + table.shape[axis + 1 :])

    def to_levels(which):
        table = jnp.concatenate(
            [half_of(vertical_modes, which, 0), half_of(mode_slopes, which, 0)], 0
        )
        return jnp.einsum("pj,zj->pz", lines, table, precision=high)

    other = lax.ppermute(to_levels(1 - part), "col", partners)
    own = to_levels(part)
    which = jnp.stack([part, scalar]).astype(jnp.int32)
    kept, passed = advance_waves(
        total, half, which, span_wavenumbers[span][None], own, other, flow
    )
    received = lax.ppermute(passed, "col", partners)
    forcing = jnp.einsum(
        "pz,jz->pj", kept, half_of(dual_modes, part, 1), precision=high
    ) + jnp.einsum("pz,jz->pj", received, half_of(dual_modes, 1 - part, 1), precision=high)
    forcing = lax.all_to_all(
        forcing.reshape(device_count, local_waves, modes), axes, 0, 0, tiled=True
    )
    forcing = jnp.swapaxes(
        forcing.reshape(scalars, spans, parts, local_waves, modes), 1, 2
    )
    zonal_waves = signed_waves(total).astype(jnp.float32) * (2.0 * math.pi / total)
    own_waves = lax.dynamic_slice_in_dim(zonal_waves, device * local_waves, local_waves)
    denominator = 1.0 + implicit_rates[:, None, None, None, None] * (
        eigenvalues[None, None, None, None, :]
        + own_waves[None, None, None, :, None] ** 2
        + span_wavenumbers[None, None, :, None, None] ** 2
    )
    return (coefficients - time_step * forcing) / denominator


def program(*arrays):
    coefficients, levels = arrays[0], arrays[3].shape[1]
    col_count = lax.axis_size("col")
    device_count = lax.axis_size("row") * col_count
    scalars, _, spans, _, _ = coefficients.shape
    fits = (
        device_count == 2 * scalars * spans
        and col_count % 2 == 0
        and (levels // 2) % lane_width == 0
        and coefficients.shape[3] * device_count == 16 * lane_width
    )
    return by_section(*arrays) if fits else on_device(*arrays)


def solution(mesh):
    in_specs = (
        P(None, None, None, ("row", "col"), None),
        P(),
        P(),
        P(),
        P(),
        P(None, "col", None),
        P(None, "col"),
        P(),
        P(),
        P(),
    )
    out_specs = P(None, None, None, ("row", "col"), None)
    return jax.shard_map(
        program, mesh=mesh, in_specs=in_specs, out_specs=out_specs, check_vma=False
    )
```
